32 devices in a mesh: groups: 2 (over x), dp: 16 (over z, y, core).
Axes of the slice: x: 2, y: 2, z: 4, core: 2. Of those that a mesh axis runs over, the one named last changes fastest.
Arguments:
- tokens: bfloat16 [128, 4096], P(('groups', 'dp')), parts along dimension 0, may hold values from -6 to 6
- target: bfloat16 [128, 4096], P(('groups', 'dp')), parts along dimension 0, may hold values from -3 to 3
- w_gate: bfloat16 [4096, 4096], P('dp'), may hold values from -0.09375 to 0.09375
- w_up: bfloat16 [4096, 4096], P('dp'), may hold values from -0.09375 to 0.09375
- w_down_t: bfloat16 [4096, 4096], P('dp'), may hold values from -0.09375 to 0.09375
- kept_blocks: int32 [30], replicated, may hold values from 0 to 31, as said below
Outputs:
- grad_gate: bfloat16 [8192, 3840], P('groups', 'dp'), parts along dimension 0
- grad_up: bfloat16 [8192, 3840], P('groups', 'dp'), parts along dimension 0
- grad_down: bfloat16 [8192, 3840], P('groups', 'dp'), parts along dimension 0
The draws below stay inside these ranges and needn't reach their ends.
There are 2 independent parts, one for each index of `groups`. The reference program is written for one: setup_inputs(seed, part) draws one part's arguments, and reference() takes and returns one part's arrays. A program takes and returns all parts, laid end to end along the dimension named above; an argument that names none is the same for every part. Nothing has to cross between parts.
Inputs may be any that keep to these rules, and one draw needn't show every extreme that they name: `kept_blocks`: distinct teacher block numbers in increasing order; blocks 0 and 31 are always kept.
All inputs are finite; a program needn't handle non-finite values.
Results may differ from the reference program's by a relative error of at most 0.0064.
Values may be sent and summed in bfloat16 or wider, within the bound.
A program may use at most 128 MiB of HBM per device.

```python
import jax
import jax.numpy as jnp
from jax import lax

D = 4096
BLK = 128
TOKENS = 64
NB = 32
FT = 4096
KB = 30
FS = 3840


def draw_kept_blocks(key, part):
    key = jax.random.fold_in(key, 11)
    inner = jax.random.permutation(key, NB - 2)[:KB - 2].astype(jnp.int32) + 1
    first = jnp.zeros((1,), jnp.int32)
    final = jnp.full((1,), NB - 1, jnp.int32)
    return jnp.sort(jnp.concatenate([first, inner, final]))


def levels(own_key, dims, shards, low, top_value):
    gain = 1.0
    for dim, parts in shards:
        draws = jax.random.uniform(jax.random.fold_in(jax.random.fold_in(own_key, 6), dim), (parts,), jnp.float32, low / len(shards), top_value / len(shards))
        gain = gain * jnp.repeat(jnp.exp(draws), dims[dim] // parts).reshape((-1,) + (1,) * (len(dims) - 1 - dim))
    return gain


def bell_draw(key, dims, deviation, most, shards=(), kind=jnp.bfloat16):
    loudness = levels(key, dims, shards, -0.22, 0.18) if shards else 1.0
    entries = jax.random.normal(key, dims, jnp.float32) * deviation * loudness
    return jnp.minimum(jnp.maximum(entries, -most), most).astype(kind)


def setup_inputs(seed: int = 0, part: int = 0) -> dict:
    splits = jax.random.split(jax.random.key(seed), 7)
    part_splits = jax.random.split(jax.random.fold_in(splits[6], part), 7)
    return {
        "tokens": bell_draw(part_splits[0], (TOKENS, D), 1.0, 6.0, ((0, 16),)),
        "target": bell_draw(part_splits[1], (TOKENS, D), 0.5, 3.0, ((0, 16),)),
        "w_gate": bell_draw(splits[2], (D, FT), D ** -0.5, 0.09375, ((0, 16),)),
        "w_up": bell_draw(splits[3], (D, FT), D ** -0.5, 0.09375, ((0, 16),)),
        "w_down_t": bell_draw(splits[4], (D, FT), FS ** -0.5, 0.09375, ((0, 16),)),
        "kept_blocks": draw_kept_blocks(jax.random.fold_in(splits[6], 71), part),
    }


LOSS_SCALE = 16.0


def channel_index(kept_blocks):
    offsets = jnp.arange(BLK, dtype=jnp.int32)
    return (kept_blocks[:, None].astype(jnp.int32) * BLK + offsets[None, :]).reshape(-1)


def reference(tokens, target, w_gate, w_up, w_down_t, kept_blocks):
    channels = channel_index(kept_blocks)
    student_gate = jnp.take(w_gate, channels, axis=1)
    student_up = jnp.take(w_up, channels, axis=1)
    student_down = jnp.take(w_down_t, channels, axis=1)
    gate_act = jnp.dot(tokens, student_gate, preferred_element_type=jnp.float32)
    up_act = jnp.dot(tokens, student_up, preferred_element_type=jnp.float32)
    sigmoid_gate = jax.nn.sigmoid(gate_act)
    silu_gate = gate_act * sigmoid_gate
    hidden = (silu_gate * up_act).astype(jnp.bfloat16)
    output = lax.dot_general(hidden, student_down, (((1,), (1,)), ((), ())), preferred_element_type=jnp.float32)
    scale = LOSS_SCALE / tokens.shape[0]
    residual = ((output - target.astype(jnp.float32)) * scale).astype(jnp.bfloat16)
    grad_down = lax.dot_general(residual, hidden, (((0,), (0,)), ((), ())), preferred_element_type=jnp.float32)
    hidden_grad = jnp.dot(residual, student_down, preferred_element_type=jnp.float32)
    slope = sigmoid_gate * (1.0 + gate_act * (1.0 - sigmoid_gate))
    gate_grad = (hidden_grad * up_act * slope).astype(jnp.bfloat16)
    up_grad = (hidden_grad * silu_gate).astype(jnp.bfloat16)
    grad_gate = lax.dot_general(tokens, gate_grad, (((0,), (0,)), ((), ())), preferred_element_type=jnp.float32)
    grad_up = lax.dot_general(tokens, up_grad, (((0,), (0,)), ((), ())), preferred_element_type=jnp.float32)
    return (grad_gate.astype(jnp.bfloat16), grad_up.astype(jnp.bfloat16), grad_down.astype(jnp.bfloat16))
```

```python
import jax
import jax.numpy as jnp
from jax import lax
from jax.sharding import PartitionSpec as P

BLK = 128


LOSS_SCALE = 16.0


def channel_index(kept_blocks):
    offsets = jnp.arange(BLK, dtype=jnp.int32)
    return (kept_blocks[:, None] * BLK + offsets[None, :]).reshape(-1)


def gathered_weights_body(tokens, target, w_gate, w_up, w_down_t, kept_blocks):
    channels = channel_index(kept_blocks)
    picked_gate = jnp.take(w_gate, channels, axis=1)
    picked_up = jnp.take(w_up, channels, axis=1)
    picked_down = jnp.take(w_down_t, channels, axis=1)
    student_gate, student_up, student_down = (
        lax.all_to_all(picked_gate, "dp", split_axis=1, concat_axis=0, tiled=True),
        lax.all_to_all(picked_up, "dp", split_axis=1, concat_axis=0, tiled=True),
        lax.all_to_all(picked_down, "dp", split_axis=1, concat_axis=0, tiled=True),
    )
    gathered = lax.all_gather(tokens, "dp", axis=0, tiled=True)
    scale = LOSS_SCALE / gathered.shape[0]
    gate_act = jnp.dot(gathered, student_gate, preferred_element_type=jnp.float32)
    up_act = jnp.dot(gathered, student_up, preferred_element_type=jnp.float32)
    sigmoid_gate = jax.nn.sigmoid(gate_act)
    silu_gate = gate_act * sigmoid_gate
    hidden = (silu_gate * up_act).astype(jnp.bfloat16)
    output_rows = lax.psum_scatter(
        lax.dot_general(
            hidden, student_down, (((1,), (1,)), ((), ())), preferred_element_type=jnp.float32
        ),
        "dp",
        scatter_dimension=0,
        tiled=True,
    )
    residual = ((output_rows - target.astype(jnp.float32)) * scale).astype(jnp.bfloat16)
    residual_all = lax.all_gather(residual, "dp", axis=0, tiled=True)
    grad_down = lax.dot_general(
        residual_all, hidden, (((0,), (0,)), ((), ())), preferred_element_type=jnp.float32
    )
    hidden_grad = jnp.dot(residual_all, student_down, preferred_element_type=jnp.float32)
    slope = sigmoid_gate * (1.0 + gate_act * (1.0 - sigmoid_gate))
    gate_grad = (hidden_grad * up_act * slope).astype(jnp.bfloat16)
    up_grad = (hidden_grad * silu_gate).astype(jnp.bfloat16)
    grad_gate = lax.dot_general(
        gathered, gate_grad, (((0,), (0,)), ((), ())), preferred_element_type=jnp.float32
    )
    grad_up = lax.dot_general(
        gathered, up_grad, (((0,), (0,)), ((), ())), preferred_element_type=jnp.float32
    )
    return (
        grad_gate.astype(jnp.bfloat16),
        grad_up.astype(jnp.bfloat16),
        grad_down.astype(jnp.bfloat16),
    )


def select_blocks(full, kept_blocks):
    rows, width = full.shape
    blocks = full.reshape(rows, width // BLK, BLK)
    return jnp.take(blocks, kept_blocks, axis=1, mode="clip").reshape(rows, -1)


def resident_weights_body(tokens, target, w_gate, w_up, w_down_t, kept_blocks):
    parts = lax.axis_size("dp")
    me = lax.axis_index("dp")
    features = w_gate.shape[0]
    held = kept_blocks.shape[0] * BLK // parts
    gathered = lax.all_gather(tokens, "dp", axis=0, tiled=True)
    rows = gathered.shape[0]
    target_slice = lax.all_to_all(target, "dp", split_axis=1, concat_axis=0, tiled=True)
    scale = LOSS_SCALE / rows
    token_slice = lax.dynamic_slice_in_dim(gathered, me * features, features, axis=1)

    def partial(left, weight):
        full = jnp.dot(left, weight, preferred_element_type=jnp.float32)
        picked = select_blocks(full.astype(jnp.bfloat16), kept_blocks)
        return picked.reshape(rows, parts, held).transpose(1, 0, 2)

    def add_up(pieces):
        moved = lax.all_to_all(pieces, "dp", split_axis=0, concat_axis=0, tiled=True)
        return jnp.sum(moved.astype(jnp.float32), axis=0)

    both = add_up(
        jnp.concatenate([partial(token_slice, w_gate), partial(token_slice, w_up)], axis=1)
    )
    gate_act, up_act = both[:rows], both[rows:]
    sigmoid_gate = jax.nn.sigmoid(gate_act)
    silu_gate = gate_act * sigmoid_gate
    hidden = (silu_gate * up_act).astype(jnp.bfloat16)
    hidden_all = lax.all_gather(hidden, "dp", axis=1, tiled=True)
    student_down = select_blocks(w_down_t, kept_blocks)
    output = lax.dot_general(
        hidden_all, student_down, (((1,), (1,)), ((), ())), preferred_element_type=jnp.float32
    )
    residual = ((output - target_slice.astype(jnp.float32)) * scale).astype(jnp.bfloat16)
    residual_all = lax.all_gather(residual, "dp", axis=1, tiled=True)
    hidden_grad = add_up(partial(residual, w_down_t))
    grad_down = lax.dot_general(
        residual_all, hidden, (((0,), (0,)), ((), ())), preferred_element_type=jnp.float32
    )
    slope = sigmoid_gate * (1.0 + gate_act * (1.0 - sigmoid_gate))
    gate_grad = (hidden_grad * up_act * slope).astype(jnp.bfloat16)
    up_grad = (hidden_grad * silu_gate).astype(jnp.bfloat16)
    grad_gate = lax.dot_general(
        gathered, gate_grad, (((0,), (0,)), ((), ())), preferred_element_type=jnp.float32
    )
    grad_up = lax.dot_general(
        gathered, up_grad, (((0,), (0,)), ((), ())), preferred_element_type=jnp.float32
    )
    return (
        grad_gate.astype(jnp.bfloat16),
        grad_up.astype(jnp.bfloat16),
        grad_down.astype(jnp.bfloat16),
    )


def body(tokens, target, w_gate, w_up, w_down_t, kept_blocks):
    token_rows = tokens.shape[0] * lax.axis_size("dp")
    few_tokens = token_rows < w_gate.shape[0]
    chosen = resident_weights_body if few_tokens else gathered_weights_body
    return chosen(tokens, target, w_gate, w_up, w_down_t, kept_blocks)


def solution(mesh):
    placed = (
        P(("groups", "dp"), None),
        P(("groups", "dp"), None),
        P("dp", None),
        P("dp", None),
        P("dp", None),
        P(),
    )
    return jax.shard_map(
        body,
        mesh=mesh,
        in_specs=placed,
        out_specs=(P("groups", "dp"), P("groups", "dp"), P("groups", "dp")),
        check_vma=False,
    )
```

```python
import functools

import jax
import jax.numpy as jnp
from jax import lax
from jax.experimental import pallas as pl
from jax.experimental.pallas import tpu as pltpu
from jax.sharding import PartitionSpec as P

BLK = 128


LOSS_SCALE = 16.0


def channel_index(kept_blocks):
    offsets = jnp.arange(BLK, dtype=jnp.int32)
    return (kept_blocks[:, None] * BLK + offsets[None, :]).reshape(-1)


def gathered_weights_body(tokens, target, w_gate, w_up, w_down_t, kept_blocks):
    channels = channel_index(kept_blocks)
    picked_gate = jnp.take(w_gate, channels, axis=1)
    picked_up = jnp.take(w_up, channels, axis=1)
    picked_down = jnp.take(w_down_t, channels, axis=1)
    student_gate, student_up, student_down = (
        lax.all_to_all(picked_gate, "dp", split_axis=1, concat_axis=0, tiled=True),
        lax.all_to_all(picked_up, "dp", split_axis=1, concat_axis=0, tiled=True),
        lax.all_to_all(picked_down, "dp", split_axis=1, concat_axis=0, tiled=True),
    )
    gathered = lax.all_gather(tokens, "dp", axis=0, tiled=True)
    scale = LOSS_SCALE / gathered.shape[0]
    gate_act = jnp.dot(gathered, student_gate, preferred_element_type=jnp.float32)
    up_act = jnp.dot(gathered, student_up, preferred_element_type=jnp.float32)
    sigmoid_gate = jax.nn.sigmoid(gate_act)
    silu_gate = gate_act * sigmoid_gate
    hidden = (silu_gate * up_act).astype(jnp.bfloat16)
    output_rows = lax.psum_scatter(
        lax.dot_general(
            hidden, student_down, (((1,), (1,)), ((), ())), preferred_element_type=jnp.float32
        ),
        "dp",
        scatter_dimension=0,
        tiled=True,
    )
    residual = ((output_rows - target.astype(jnp.float32)) * scale).astype(jnp.bfloat16)
    residual_all = lax.all_gather(residual, "dp", axis=0, tiled=True)
    grad_down = lax.dot_general(
        residual_all, hidden, (((0,), (0,)), ((), ())), preferred_element_type=jnp.float32
    )
    hidden_grad = jnp.dot(residual_all, student_down, preferred_element_type=jnp.float32)
    slope = sigmoid_gate * (1.0 + gate_act * (1.0 - sigmoid_gate))
    gate_grad = (hidden_grad * up_act * slope).astype(jnp.bfloat16)
    up_grad = (hidden_grad * silu_gate).astype(jnp.bfloat16)
    grad_gate = lax.dot_general(
        gathered, gate_grad, (((0,), (0,)), ((), ())), preferred_element_type=jnp.float32
    )
    grad_up = lax.dot_general(
        gathered, up_grad, (((0,), (0,)), ((), ())), preferred_element_type=jnp.float32
    )
    return (
        grad_gate.astype(jnp.bfloat16),
        grad_up.astype(jnp.bfloat16),
        grad_down.astype(jnp.bfloat16),
    )


def exchange_kernel(
    n, held, kept, packed, wg_hbm, wu_hbm, wd_hbm, gate_out, up_out, hid_out, tok_all, res_all,
    wg, wu, wd, packs, tok32, tgt32, tok16, full, sel, down32, down, act_out, act_in,
    hid16, hid_in, res16, hg_out, hg_in, load_sem, send_sem, recv_sem,
):
    me = lax.axis_index("dp")
    rows, features = tok16.shape
    wide = hid16.shape[1]
    kept_count = kept.shape[0]
    mine = rows // n
    bf16, f32 = jnp.bfloat16, jnp.float32

    loads = [
        pltpu.make_async_copy(src, dst, load_sem.at[i])
        for i, (src, dst) in enumerate(((wg_hbm, wg), (wu_hbm, wu), (wd_hbm, wd)))
    ]
    for load in loads:
        load.start()

    barrier = pltpu.get_barrier_semaphore()

    @pl.loop(1, n)
    def _(k):
        pl.semaphore_signal(
            barrier, inc=1, device_id={"dp": lax.rem(me + k, n)},
            device_id_type=pl.DeviceIdType.MESH,
        )

    pl.semaphore_wait(barrier, n - 1)

    def remote(phase, k, src, dst):
        return pltpu.make_async_remote_copy(
            src_ref=src, dst_ref=dst, send_sem=send_sem.at[phase, k],
            recv_sem=recv_sem.at[phase, k], device_id={"dp": lax.rem(me + k, n)},
            device_id_type=pl.DeviceIdType.MESH,
        )

    def columns(index):
        return pl.ds(pl.multiple_of(index * features, features), features)

    def pack_copy(k):
        return remote(0, k, packed.at[:, columns(lax.rem(me + k, n))], packs.at[me])

    def act_copy(k):
        return remote(1, k, act_out.at[lax.rem(me + k, n)], act_in.at[me])

    def hid_copy(k):
        return remote(2, k, hid16, hid_in.at[me])

    def res_copy(k):
        return remote(3, k, res16, res_all.at[:, columns(me)])

    def hg_copy(k):
        return remote(4, k, hg_out.at[lax.rem(me + k, n)], hg_in.at[me])

    def tok_copy(k):
        return remote(5, k, tok16, tok_all.at[:, columns(me)])

    spare = wd.shape[1] // BLK - kept_count

    def kept_block(ref, b):
        shift = jnp.full((ref.shape[0], BLK), kept[b] - b, jnp.int32)
        chosen = ref[:, b * BLK:(b + 1) * BLK].astype(f32)
        for j in range(1, spare + 1):
            other = ref[:, (b + j) * BLK:(b + j + 1) * BLK].astype(f32)
            chosen = jnp.where(shift == j, other, chosen)
        return chosen

    def start_all(copy):
        @pl.loop(1, n)
        def _(k):
            copy(k).start()

    def receive_all(copy):
        @pl.loop(1, n)
        def _(k):
            copy(k).wait_recv()

    def sent_all(copy):
        @pl.loop(1, n)
        def _(k):
            copy(k).wait_send()

    start_all(pack_copy)
    packs[me] = packed[:, columns(me)]
    receive_all(pack_copy)
    for s in range(n):
        piece = packs[s].astype(f32)
        tok32[s * mine:(s + 1) * mine, :] = piece[:mine]
        tgt32[s * mine:(s + 1) * mine, :] = piece[mine:2 * mine]
    tok16[...] = tok32[...].astype(bf16)

    loads[0].wait()
    loads[1].wait()
    for half, weight in enumerate((wg, wu)):
        here = pl.ds(half * rows, rows)
        for c in range(0, weight.shape[1], 512):
            full[here, c:c + 512] = jnp.dot(
                tok16[...], weight[:, c:c + 512], preferred_element_type=f32
            )
    sel[:, kept_count * BLK:] = jnp.zeros((2 * rows, BLK), f32)
    for b in range(kept_count):
        sel[:, b * BLK:(b + 1) * BLK] = kept_block(full, b)
    for p in range(n):
        act_out[p] = sel[:, p * held:p * held + wide].astype(bf16)
    start_all(act_copy)
    act_in[me] = act_out[me]
    start_all(tok_copy)
    tok_all[:, columns(me)] = tok16[...]

    loads[2].wait()
    down32[:, kept_count * BLK:] = jnp.zeros((features, BLK), f32)
    for b in range(kept_count):
        down32[:, b * BLK:(b + 1) * BLK] = kept_block(wd, b)
    for p in range(n):
        down[p] = down32[:, p * held:p * held + wide].astype(bf16)

    receive_all(act_copy)
    both = act_in[0].astype(f32)
    for s in range(1, n):
        both = both + act_in[s].astype(f32)
    gate_act, up_act = both[:rows], both[rows:]
    sigmoid_gate = jax.nn.sigmoid(gate_act)
    silu_gate = gate_act * sigmoid_gate
    inside = lax.broadcasted_iota(jnp.int32, (rows, wide), 1) < held
    hidden = jnp.where(inside, silu_gate * up_act, 0.0).astype(bf16)
    hid16[...] = hidden
    hid_out[...] = hidden
    start_all(hid_copy)
    hid_in[me] = hidden
    receive_all(hid_copy)

    output = jnp.zeros((rows, features), f32)
    for s in range(n):
        output = output + lax.dot_general(
            hid_in[s], down[s], (((1,), (1,)), ((), ())), preferred_element_type=f32
        )
    residual = ((output - tgt32[...]) * (LOSS_SCALE / rows)).astype(bf16)
    res16[...] = residual

    @pl.loop(1, n)
    def _(k):
        p = lax.rem(me + k, n)
        hg_out[p] = jnp.dot(res16[...], down[p], preferred_element_type=f32).astype(bf16)
        hg_copy(k).start()

    hg_in[me] = jnp.dot(res16[...], down[me], preferred_element_type=f32).astype(bf16)
    start_all(res_copy)
    res_all[:, columns(me)] = residual
    receive_all(hg_copy)
    hidden_grad = hg_in[0].astype(f32)
    for s in range(1, n):
        hidden_grad = hidden_grad + hg_in[s].astype(f32)
    slope = sigmoid_gate * (1.0 + gate_act * (1.0 - sigmoid_gate))
    gate_out[...] = (hidden_grad * up_act * slope).astype(bf16)
    up_out[...] = (hidden_grad * silu_gate).astype(bf16)

    receive_all(tok_copy)
    receive_all(res_copy)
    for copy in (pack_copy, act_copy, hid_copy, res_copy, hg_copy, tok_copy):
        sent_all(copy)


def resident_weights_body(tokens, target, w_gate, w_up, w_down_t, kept_blocks):
    n = lax.axis_size("dp")
    mine, width = tokens.shape
    rows = mine * n
    features, channels = w_gate.shape
    kept_count = kept_blocks.shape[0]
    held = kept_count * BLK // n
    wide = -(-held // BLK) * BLK
    pack_rows = -(-2 * mine // 16) * 16
    filler = jnp.zeros((pack_rows - 2 * mine, width), tokens.dtype)
    packed = jnp.concatenate([tokens, target, filler], axis=0)
    bf16, f32 = jnp.bfloat16, jnp.float32
    vmem = pl.BlockSpec(memory_space=pltpu.VMEM)
    hbm = pl.BlockSpec(memory_space=pl.ANY)
    small = jax.ShapeDtypeStruct((rows, wide), bf16)
    large = jax.ShapeDtypeStruct((rows, width), bf16)
    picked = kept_count * BLK + BLK
    gate_grad, up_grad, hidden, tok_all, res_all = pl.pallas_call(
        functools.partial(exchange_kernel, n, held),
        out_shape=(small, small, small, large, large),
        in_specs=[pl.BlockSpec(memory_space=pltpu.SMEM), vmem, hbm, hbm, hbm],
        out_specs=(vmem,) * 5,
        scratch_shapes=[
            pltpu.VMEM((features, channels), bf16),
            pltpu.VMEM((features, channels), bf16),
            pltpu.VMEM((features, channels), bf16),
            pltpu.VMEM((n, pack_rows, features), bf16),
            pltpu.VMEM((rows, features), f32),
            pltpu.VMEM((rows, features), f32),
            pltpu.VMEM((rows, features), bf16),
            pltpu.VMEM((2 * rows, channels), f32),
            pltpu.VMEM((2 * rows, picked), f32),
            pltpu.VMEM((features, picked), f32),
            pltpu.VMEM((n, features, wide), bf16),
            pltpu.VMEM((n, 2 * rows, wide), bf16),
            pltpu.VMEM((n, 2 * rows, wide), bf16),
            pltpu.VMEM((rows, wide), bf16),
            pltpu.VMEM((n, rows, wide), bf16),
            pltpu.VMEM((rows, features), bf16),
            pltpu.VMEM((n, rows, wide), bf16),
            pltpu.VMEM((n, rows, wide), bf16),
            pltpu.SemaphoreType.DMA((3,)),
            pltpu.SemaphoreType.DMA((6, n)),
            pltpu.SemaphoreType.DMA((6, n)),
        ],
        compiler_params=pltpu.CompilerParams(
            collective_id=0, has_side_effects=True, vmem_limit_bytes=44 * 1024 * 1024
        ),
    )(kept_blocks, packed, w_gate, w_up, w_down_t)

    def over_tokens(left, right):
        product = lax.dot_general(
            left, right[:, :held], (((0,), (0,)), ((), ())), preferred_element_type=f32
        )
        return product.astype(bf16)

    return (
        over_tokens(tok_all, gate_grad),
        over_tokens(tok_all, up_grad),
        over_tokens(res_all, hidden),
    )


def body(tokens, target, w_gate, w_up, w_down_t, kept_blocks):
    token_rows = tokens.shape[0] * lax.axis_size("dp")
    few_tokens = token_rows < w_gate.shape[0]
    few_dropped = w_gate.shape[1] // BLK - kept_blocks.shape[0] <= 4
    chosen = resident_weights_body if few_tokens and few_dropped else gathered_weights_body
    return chosen(tokens, target, w_gate, w_up, w_down_t, kept_blocks)


def solution(mesh):
    placed = (
        P(("groups", "dp"), None),
        P(("groups", "dp"), None),
        P("dp", None),
        P("dp", None),
        P("dp", None),
        P(),
    )
    return jax.shard_map(
        body,
        mesh=mesh,
        in_specs=placed,
        out_specs=(P("groups", "dp"), P("groups", "dp"), P("groups", "dp")),
        check_vma=False,
    )
```

```python
import functools

import jax
import jax.numpy as jnp
from jax import lax
from jax.experimental import pallas as pl
from jax.experimental.pallas import tpu as pltpu
from jax.sharding import PartitionSpec as P

BLK = 128


LOSS_SCALE = 16.0


def channel_index(kept_blocks):
    offsets = jnp.arange(BLK, dtype=jnp.int32)
    return (kept_blocks[:, None] * BLK + offsets[None, :]).reshape(-1)


def gathered_weights_body(tokens, target, w_gate, w_up, w_down_t, kept_blocks):
    channels = channel_index(kept_blocks)
    picked_gate = jnp.take(w_gate, channels, axis=1)
    picked_up = jnp.take(w_up, channels, axis=1)
    picked_down = jnp.take(w_down_t, channels, axis=1)
    student_gate, student_up, student_down = (
        lax.all_to_all(picked_gate, "dp", split_axis=1, concat_axis=0, tiled=True),
        lax.all_to_all(picked_up, "dp", split_axis=1, concat_axis=0, tiled=True),
        lax.all_to_all(picked_down, "dp", split_axis=1, concat_axis=0, tiled=True),
    )
    gathered = lax.all_gather(tokens, "dp", axis=0, tiled=True)
    scale = LOSS_SCALE / gathered.shape[0]
    gate_act = jnp.dot(gathered, student_gate, preferred_element_type=jnp.float32)
    up_act = jnp.dot(gathered, student_up, preferred_element_type=jnp.float32)
    sigmoid_gate = jax.nn.sigmoid(gate_act)
    silu_gate = gate_act * sigmoid_gate
    hidden = (silu_gate * up_act).astype(jnp.bfloat16)
    output_rows = lax.psum_scatter(
        lax.dot_general(
            hidden, student_down, (((1,), (1,)), ((), ())), preferred_element_type=jnp.float32
        ),
        "dp",
        scatter_dimension=0,
        tiled=True,
    )
    residual = ((output_rows - target.astype(jnp.float32)) * scale).astype(jnp.bfloat16)
    residual_all = lax.all_gather(residual, "dp", axis=0, tiled=True)
    grad_down = lax.dot_general(
        residual_all, hidden, (((0,), (0,)), ((), ())), preferred_element_type=jnp.float32
    )
    hidden_grad = jnp.dot(residual_all, student_down, preferred_element_type=jnp.float32)
    slope = sigmoid_gate * (1.0 + gate_act * (1.0 - sigmoid_gate))
    gate_grad = (hidden_grad * up_act * slope).astype(jnp.bfloat16)
    up_grad = (hidden_grad * silu_gate).astype(jnp.bfloat16)
    grad_gate = lax.dot_general(
        gathered, gate_grad, (((0,), (0,)), ((), ())), preferred_element_type=jnp.float32
    )
    grad_up = lax.dot_general(
        gathered, up_grad, (((0,), (0,)), ((), ())), preferred_element_type=jnp.float32
    )
    return (
        grad_gate.astype(jnp.bfloat16),
        grad_up.astype(jnp.bfloat16),
        grad_down.astype(jnp.bfloat16),
    )


def exchange_kernel(
    n, held, kept, packed, wg_hbm, wu_hbm, wd_hbm, gate_out, up_out, hid_out, tok_all, res_all,
    wg, wu, wd, packs, tok32, tgt32, tok16, full, sel, down32, down, act_out, act_in,
    hid16, hid_in, res16, hg_out, hg_in, load_sem, send_sem, recv_sem,
):
    me = lax.axis_index("dp")
    rows, features = tok16.shape
    wide = hid16.shape[1]
    kept_count = kept.shape[0]
    mine = rows // n
    bf16, f32 = jnp.bfloat16, jnp.float32

    loads = [
        pltpu.make_async_copy(src, dst, load_sem.at[i])
        for i, (src, dst) in enumerate(((wg_hbm, wg), (wu_hbm, wu), (wd_hbm, wd)))
    ]
    for load in loads:
        load.start()

    barrier = pltpu.get_barrier_semaphore()

    @pl.loop(1, n)
    def _(k):
        pl.semaphore_signal(
            barrier, inc=1, device_id={"dp": lax.rem(me + k, n)},
            device_id_type=pl.DeviceIdType.MESH,
        )

    pl.semaphore_wait(barrier, n - 1)

    def remote(phase, k, src, dst, to=None):
        return pltpu.make_async_remote_copy(
            src_ref=src, dst_ref=dst, send_sem=send_sem.at[phase, k],
            recv_sem=recv_sem.at[phase, k],
            device_id={"dp": lax.rem(me + k, n) if to is None else to},
            device_id_type=pl.DeviceIdType.MESH,
        )

    chips = n // 2
    sibling = me + 1 - 2 * lax.rem(me, 2)

    def gather_copies(phase, own, slot):
        def across(k):
            return remote(phase, k, own, slot(me), lax.rem(me + 2 * k, n))

        def beside():
            return remote(phase, 0, own, slot(me), sibling)

        def onward(k):
            held_slot = slot(lax.rem(me + n - 2 * k, n))
            return remote(phase, chips + k, held_slot, held_slot, sibling)

        def start():
            @pl.loop(1, chips)
            def _(k):
                across(k).start()

            beside().start()

        def forward():
            @pl.loop(1, chips)
            def _(k):
                across(k).wait_recv()
                onward(k).start()

        def finish():
            beside().wait_recv()

            @pl.loop(1, chips)
            def _(k):
                onward(k).wait_recv()

        def sent():
            beside().wait_send()

            @pl.loop(1, chips)
            def _(k):
                across(k).wait_send()
                onward(k).wait_send()

        return start, forward, finish, sent

    def columns(index):
        return pl.ds(pl.multiple_of(index * features, features), features)

    def pack_copy(k):
        return remote(0, k, packed.at[:, columns(lax.rem(me + k, n))], packs.at[me])

    def act_copy(k):
        return remote(1, k, act_out.at[lax.rem(me + k, n)], act_in.at[me])

    def hg_copy(k):
        return remote(4, k, hg_out.at[lax.rem(me + k, n)], hg_in.at[me])

    hid_start, hid_forward, hid_finish, hid_sent = gather_copies(
        2, hid16, lambda i: hid_in.at[i]
    )
    res_start, res_forward, res_finish, res_sent = gather_copies(
        3, res16, lambda i: res_all.at[:, columns(i)]
    )
    tok_start, tok_forward, tok_finish, tok_sent = gather_copies(
        5, tok16, lambda i: tok_all.at[:, columns(i)]
    )

    spare = wd.shape[1] // BLK - kept_count

    def kept_block(ref, b):
        shift = jnp.full((ref.shape[0], BLK), kept[b] - b, jnp.int32)
        chosen = ref[:, b * BLK:(b + 1) * BLK].astype(f32)
        for j in range(1, spare + 1):
            other = ref[:, (b + j) * BLK:(b + j + 1) * BLK].astype(f32)
            chosen = jnp.where(shift == j, other, chosen)
        return chosen

    def start_all(copy):
        @pl.loop(1, n)
        def _(k):
            copy(k).start()

    def receive_all(copy):
        @pl.loop(1, n)
        def _(k):
            copy(k).wait_recv()

    def sent_all(copy):
        @pl.loop(1, n)
        def _(k):
            copy(k).wait_send()

    start_all(pack_copy)
    packs[me] = packed[:, columns(me)]
    receive_all(pack_copy)
    for s in range(n):
        piece = packs[s].astype(f32)
        tok32[s * mine:(s + 1) * mine, :] = piece[:mine]
        tgt32[s * mine:(s + 1) * mine, :] = piece[mine:2 * mine]
    tok16[...] = tok32[...].astype(bf16)
    tok_start()

    loads[0].wait()
    loads[1].wait()
    for half, weight in enumerate((wg, wu)):
        here = pl.ds(half * rows, rows)
        for c in range(0, weight.shape[1], 512):
            full[here, c:c + 512] = jnp.dot(
                tok16[...], weight[:, c:c + 512], preferred_element_type=f32
            )
    sel[:, kept_count * BLK:] = jnp.zeros((2 * rows, BLK), f32)
    for b in range(kept_count):
        sel[:, b * BLK:(b + 1) * BLK] = kept_block(full, b)
    for p in range(n):
        act_out[p] = sel[:, p * held:p * held + wide].astype(bf16)
    start_all(act_copy)
    act_in[me] = act_out[me]
    tok_all[:, columns(me)] = tok16[...]

    loads[2].wait()
    down32[:, kept_count * BLK:] = jnp.zeros((features, BLK), f32)
    for b in range(kept_count):
        down32[:, b * BLK:(b + 1) * BLK] = kept_block(wd, b)
    for p in range(n):
        down[p] = down32[:, p * held:p * held + wide].astype(bf16)

    tok_forward()
    receive_all(act_copy)
    both = act_in[0].astype(f32)
    for s in range(1, n):
        both = both + act_in[s].astype(f32)
    gate_act, up_act = both[:rows], both[rows:]
    sigmoid_gate = jax.nn.sigmoid(gate_act)
    silu_gate = gate_act * sigmoid_gate
    inside = lax.broadcasted_iota(jnp.int32, (rows, wide), 1) < held
    hidden = jnp.where(inside, silu_gate * up_act, 0.0).astype(bf16)
    hid16[...] = hidden
    hid_out[...] = hidden
    hid_start()
    hid_in[me] = hidden
    hid_forward()
    hid_finish()

    output = jnp.zeros((rows, features), f32)
    for s in range(n):
        output = output + lax.dot_general(
            hid_in[s], down[s], (((1,), (1,)), ((), ())), preferred_element_type=f32
        )
    residual = ((output - tgt32[...]) * (LOSS_SCALE / rows)).astype(bf16)
    res16[...] = residual

    @pl.loop(1, n)
    def _(k):
        p = lax.rem(me + k, n)
        hg_out[p] = jnp.dot(res16[...], down[p], preferred_element_type=f32).astype(bf16)
        hg_copy(k).start()

    hg_in[me] = jnp.dot(res16[...], down[me], preferred_element_type=f32).astype(bf16)
    res_start()
    res_all[:, columns(me)] = residual
    res_forward()
    receive_all(hg_copy)
    hidden_grad = hg_in[0].astype(f32)
    for s in range(1, n):
        hidden_grad = hidden_grad + hg_in[s].astype(f32)
    slope = sigmoid_gate * (1.0 + gate_act * (1.0 - sigmoid_gate))
    gate_out[...] = (hidden_grad * up_act * slope).astype(bf16)
    up_out[...] = (hidden_grad * silu_gate).astype(bf16)

    tok_finish()
    res_finish()
    for copy in (pack_copy, act_copy, hg_copy):
        sent_all(copy)
    for sent in (tok_sent, hid_sent, res_sent):
        sent()


def resident_weights_body(tokens, target, w_gate, w_up, w_down_t, kept_blocks):
    n = lax.axis_size("dp")
    mine, width = tokens.shape
    rows = mine * n
    features, channels = w_gate.shape
    kept_count = kept_blocks.shape[0]
    held = kept_count * BLK // n
    wide = -(-held // BLK) * BLK
    pack_rows = -(-2 * mine // 16) * 16
    filler = jnp.zeros((pack_rows - 2 * mine, width), tokens.dtype)
    packed = jnp.concatenate([tokens, target, filler], axis=0)
    bf16, f32 = jnp.bfloat16, jnp.float32
    vmem = pl.BlockSpec(memory_space=pltpu.VMEM)
    hbm = pl.BlockSpec(memory_space=pltpu.HBM)
    small = jax.ShapeDtypeStruct((rows, wide), bf16)
    large = jax.ShapeDtypeStruct((rows, width), bf16)
    picked = kept_count * BLK + BLK
    gate_grad, up_grad, hidden, tok_all, res_all = pl.pallas_call(
        functools.partial(exchange_kernel, n, held),
        out_shape=(small, small, small, large, large),
        in_specs=[pl.BlockSpec(memory_space=pltpu.SMEM), vmem, hbm, hbm, hbm],
        out_specs=(vmem,) * 5,
        scratch_shapes=[
            pltpu.VMEM((features, channels), bf16),
            pltpu.VMEM((features, channels), bf16),
            pltpu.VMEM((features, channels), bf16),
            pltpu.VMEM((n, pack_rows, features), bf16),
            pltpu.VMEM((rows, features), f32),
            pltpu.VMEM((rows, features), f32),
            pltpu.VMEM((rows, features), bf16),
            pltpu.VMEM((2 * rows, channels), f32),
            pltpu.VMEM((2 * rows, picked), f32),
            pltpu.VMEM((features, picked), f32),
            pltpu.VMEM((n, features, wide), bf16),
            pltpu.VMEM((n, 2 * rows, wide), bf16),
            pltpu.VMEM((n, 2 * rows, wide), bf16),
            pltpu.VMEM((rows, wide), bf16),
            pltpu.VMEM((n, rows, wide), bf16),
            pltpu.VMEM((rows, features), bf16),
            pltpu.VMEM((n, rows, wide), bf16),
            pltpu.VMEM((n, rows, wide), bf16),
            pltpu.SemaphoreType.DMA((3,)),
            pltpu.SemaphoreType.DMA((6, n)),
            pltpu.SemaphoreType.DMA((6, n)),
        ],
        compiler_params=pltpu.CompilerParams(
            collective_id=0, has_side_effects=True, vmem_limit_bytes=58 * 1024 * 1024
        ),
    )(kept_blocks, packed, w_gate, w_up, w_down_t)

    def over_tokens(left, right):
        product = lax.dot_general(
            left, right[:, :held], (((0,), (0,)), ((), ())), preferred_element_type=f32
        )
        return product.astype(bf16)

    return (
        over_tokens(tok_all, gate_grad),
        over_tokens(tok_all, up_grad),
        over_tokens(res_all, hidden),
    )


def body(tokens, target, w_gate, w_up, w_down_t, kept_blocks):
    token_rows = tokens.shape[0] * lax.axis_size("dp")
    few_tokens = token_rows < w_gate.shape[0]
    few_dropped = w_gate.shape[1] // BLK - kept_blocks.shape[0] <= 4
    paired = lax.axis_size("dp") % 2 == 0
    resident = few_tokens and few_dropped and paired
    chosen = resident_weights_body if resident else gathered_weights_body
    return chosen(tokens, target, w_gate, w_up, w_down_t, kept_blocks)


def solution(mesh):
    placed = (
        P(("groups", "dp"), None),
        P(("groups", "dp"), None),
        P("dp", None),
        P("dp", None),
        P("dp", None),
        P(),
    )
    return jax.shard_map(
        body,
        mesh=mesh,
        in_specs=placed,
        out_specs=(P("groups", "dp"), P("groups", "dp"), P("groups", "dp")),
        check_vma=False,
    )
```

```python
import functools

import jax
import jax.numpy as jnp
from jax import lax
from jax.experimental import pallas as pl
from jax.experimental.pallas import tpu as pltpu
from jax.sharding import PartitionSpec as P

BLK = 128


LOSS_SCALE = 16.0


def channel_index(kept_blocks):
    offsets = jnp.arange(BLK, dtype=jnp.int32)
    return (kept_blocks[:, None] * BLK + offsets[None, :]).reshape(-1)


def gathered_weights_body(tokens, target, w_gate, w_up, w_down_t, kept_blocks):
    channels = channel_index(kept_blocks)
    picked_gate = jnp.take(w_gate, channels, axis=1)
    picked_up = jnp.take(w_up, channels, axis=1)
    picked_down = jnp.take(w_down_t, channels, axis=1)
    student_gate, student_up, student_down = (
        lax.all_to_all(picked_gate, "dp", split_axis=1, concat_axis=0, tiled=True),
        lax.all_to_all(picked_up, "dp", split_axis=1, concat_axis=0, tiled=True),
        lax.all_to_all(picked_down, "dp", split_axis=1, concat_axis=0, tiled=True),
    )
    gathered = lax.all_gather(tokens, "dp", axis=0, tiled=True)
    scale = LOSS_SCALE / gathered.shape[0]
    gate_act = jnp.dot(gathered, student_gate, preferred_element_type=jnp.float32)
    up_act = jnp.dot(gathered, student_up, preferred_element_type=jnp.float32)
    sigmoid_gate = jax.nn.sigmoid(gate_act)
    silu_gate = gate_act * sigmoid_gate
    hidden = (silu_gate * up_act).astype(jnp.bfloat16)
    output_rows = lax.psum_scatter(
        lax.dot_general(
            hidden, student_down, (((1,), (1,)), ((), ())), preferred_element_type=jnp.float32
        ),
        "dp",
        scatter_dimension=0,
        tiled=True,
    )
    residual = ((output_rows - target.astype(jnp.float32)) * scale).astype(jnp.bfloat16)
    residual_all = lax.all_gather(residual, "dp", axis=0, tiled=True)
    grad_down = lax.dot_general(
        residual_all, hidden, (((0,), (0,)), ((), ())), preferred_element_type=jnp.float32
    )
    hidden_grad = jnp.dot(residual_all, student_down, preferred_element_type=jnp.float32)
    slope = sigmoid_gate * (1.0 + gate_act * (1.0 - sigmoid_gate))
    gate_grad = (hidden_grad * up_act * slope).astype(jnp.bfloat16)
    up_grad = (hidden_grad * silu_gate).astype(jnp.bfloat16)
    grad_gate = lax.dot_general(
        gathered, gate_grad, (((0,), (0,)), ((), ())), preferred_element_type=jnp.float32
    )
    grad_up = lax.dot_general(
        gathered, up_grad, (((0,), (0,)), ((), ())), preferred_element_type=jnp.float32
    )
    return (
        grad_gate.astype(jnp.bfloat16),
        grad_up.astype(jnp.bfloat16),
        grad_down.astype(jnp.bfloat16),
    )


def exchange_kernel(
    n, held, kept, packed, wg_hbm, wu_hbm, wd_hbm, gate_out, up_out, hid_out, tok_all, res_all,
    wg, wu, wd, packs, tok32, tgt32, tok16, full, sel, down32, down,
    act_out, act_pair, act_sum, act_in, hid16, hid_in, res16, hg_out, hg_pair, hg_sum, hg_in, load_sem, send_sem, recv_sem,
):
    me = lax.axis_index("dp")
    rows, features = tok16.shape
    wide = hid16.shape[1]
    kept_count = kept.shape[0]
    mine = rows // n
    bf16, f32 = jnp.bfloat16, jnp.float32

    loads = [
        pltpu.make_async_copy(src, dst, load_sem.at[i])
        for i, (src, dst) in enumerate(((wg_hbm, wg), (wu_hbm, wu), (wd_hbm, wd)))
    ]
    for load in loads:
        load.start()

    barrier = pltpu.get_barrier_semaphore()

    @pl.loop(1, n)
    def _(k):
        pl.semaphore_signal(
            barrier, inc=1, device_id={"dp": lax.rem(me + k, n)},
            device_id_type=pl.DeviceIdType.MESH,
        )

    pl.semaphore_wait(barrier, n - 1)

    def remote(phase, k, src, dst, to=None):
        return pltpu.make_async_remote_copy(
            src_ref=src, dst_ref=dst, send_sem=send_sem.at[phase, k],
            recv_sem=recv_sem.at[phase, k],
            device_id={"dp": lax.rem(me + k, n) if to is None else to},
            device_id_type=pl.DeviceIdType.MESH,
        )

    chips = n // 2
    sibling = me + 1 - 2 * lax.rem(me, 2)

    def gather_copies(phase, own, slot):
        def across(k):
            return remote(phase, k, own, slot(me), lax.rem(me + 2 * k, n))

        def beside():
            return remote(phase, 0, own, slot(me), sibling)

        def onward(k):
            held_slot = slot(lax.rem(me + n - 2 * k, n))
            return remote(phase, chips + k, held_slot, held_slot, sibling)

        def start():
            @pl.loop(1, chips)
            def _(k):
                across(k).start()

            beside().start()

        def forward():
            @pl.loop(1, chips)
            def _(k):
                across(k).wait_recv()
                onward(k).start()

        def finish():
            beside().wait_recv()

            @pl.loop(1, chips)
            def _(k):
                onward(k).wait_recv()

        def sent():
            beside().wait_send()

            @pl.loop(1, chips)
            def _(k):
                across(k).wait_send()
                onward(k).wait_send()

        return start, forward, finish, sent

    def columns(index):
        return pl.ds(pl.multiple_of(index * features, features), features)

    def pack_copy(k):
        return remote(0, k, packed.at[:, columns(lax.rem(me + k, n))], packs.at[me])

    core = lax.rem(me, 2)
    chip = lax.div(me, 2)

    def sum_copies(phase, out, pair, total, landed):
        def there(k):
            return lax.rem(chip + k, chips)

        def beside(k):
            j = there(k)
            return remote(phase, k, out.at[2 * j + 1 - core], pair.at[j], sibling)

        def across(k):
            j = there(k)
            return remote(phase, chips + k, total.at[j], landed.at[chip], 2 * j + core)

        def combine():
            @pl.loop(1, chips)
            def _(k):
                j = there(k)
                beside(k).wait_recv()
                total[j] = (out[2 * j + core] + pair[j]).astype(bf16)
                across(k).start()

            beside(0).wait_recv()
            landed[chip] = (out[me] + pair[chip]).astype(bf16)

        def finish():
            @pl.loop(1, chips)
            def _(k):
                across(k).wait_recv()

            result = landed[0].astype(f32)
            for s in range(1, chips):
                result = result + landed[s].astype(f32)
            return result

        def sent():
            beside(0).wait_send()

            @pl.loop(1, chips)
            def _(k):
                beside(k).wait_send()
                across(k).wait_send()

        return there, beside, combine, finish, sent

    _, act_beside, act_combine, act_finish, act_sent = sum_copies(
        1, act_out, act_pair, act_sum, act_in
    )
    hg_there, hg_beside, hg_combine, hg_finish, hg_sent = sum_copies(
        4, hg_out, hg_pair, hg_sum, hg_in
    )
    hid_start, hid_forward, hid_finish, hid_sent = gather_copies(
        2, hid16, lambda i: hid_in.at[i]
    )
    res_start, res_forward, res_finish, res_sent = gather_copies(
        3, res16, lambda i: res_all.at[:, columns(i)]
    )
    tok_start, tok_forward, tok_finish, tok_sent = gather_copies(
        5, tok16, lambda i: tok_all.at[:, columns(i)]
    )

    spare = wd.shape[1] // BLK - kept_count

    def kept_block(ref, b):
        shift = jnp.full((ref.shape[0], BLK), kept[b] - b, jnp.int32)
        chosen = ref[:, b * BLK:(b + 1) * BLK].astype(f32)
        for j in range(1, spare + 1):
            other = ref[:, (b + j) * BLK:(b + j + 1) * BLK].astype(f32)
            chosen = jnp.where(shift == j, other, chosen)
        return chosen

    def start_all(copy):
        @pl.loop(1, n)
        def _(k):
            copy(k).start()

    def receive_all(copy):
        @pl.loop(1, n)
        def _(k):
            copy(k).wait_recv()

    def sent_all(copy):
        @pl.loop(1, n)
        def _(k):
            copy(k).wait_send()

    start_all(pack_copy)
    packs[me] = packed[:, columns(me)]
    receive_all(pack_copy)
    for s in range(n):
        piece = packs[s].astype(f32)
        tok32[s * mine:(s + 1) * mine, :] = piece[:mine]
        tgt32[s * mine:(s + 1) * mine, :] = piece[mine:2 * mine]
    tok16[...] = tok32[...].astype(bf16)
    tok_start()

    loads[0].wait()
    loads[1].wait()
    for half, weight in enumerate((wg, wu)):
        here = pl.ds(half * rows, rows)
        for c in range(0, weight.shape[1], 512):
            full[here, c:c + 512] = jnp.dot(
                tok16[...], weight[:, c:c + 512], preferred_element_type=f32
            )
    sel[:, kept_count * BLK:] = jnp.zeros((2 * rows, BLK), f32)
    for b in range(kept_count):
        sel[:, b * BLK:(b + 1) * BLK] = kept_block(full, b)
    for p in range(n):
        act_out[p] = sel[:, p * held:p * held + wide]

    @pl.loop(1, chips)
    def _(k):
        act_beside(k).start()

    act_beside(0).start()
    act_combine()
    tok_all[:, columns(me)] = tok16[...]

    loads[2].wait()
    down32[:, kept_count * BLK:] = jnp.zeros((features, BLK), f32)
    for b in range(kept_count):
        down32[:, b * BLK:(b + 1) * BLK] = kept_block(wd, b)
    for p in range(n):
        down[p] = down32[:, p * held:p * held + wide].astype(bf16)

    tok_forward()
    both = act_finish()
    gate_act, up_act = both[:rows], both[rows:]
    sigmoid_gate = jax.nn.sigmoid(gate_act)
    silu_gate = gate_act * sigmoid_gate
    inside = lax.broadcasted_iota(jnp.int32, (rows, wide), 1) < held
    hidden = jnp.where(inside, silu_gate * up_act, 0.0).astype(bf16)
    hid16[...] = hidden
    hid_out[...] = hidden
    hid_start()
    hid_in[me] = hidden
    hid_forward()
    hid_finish()

    output = jnp.zeros((rows, features), f32)
    for s in range(n):
        output = output + lax.dot_general(
            hid_in[s], down[s], (((1,), (1,)), ((), ())), preferred_element_type=f32
        )
    residual = ((output - tgt32[...]) * (LOSS_SCALE / rows)).astype(bf16)
    res16[...] = residual

    def hg_piece(p):
        hg_out[p] = jnp.dot(res16[...], down[p], preferred_element_type=f32)

    @pl.loop(1, chips + 1)
    def _(step):
        k = lax.rem(step, chips)
        hg_piece(2 * hg_there(k) + 1 - core)
        hg_beside(k).start()

    @pl.loop(0, chips)
    def _(k):
        hg_piece(2 * hg_there(k) + core)

    hg_combine()
    res_start()
    res_all[:, columns(me)] = residual
    res_forward()
    hidden_grad = hg_finish()
    slope = sigmoid_gate * (1.0 + gate_act * (1.0 - sigmoid_gate))
    gate_out[...] = (hidden_grad * up_act * slope).astype(bf16)
    up_out[...] = (hidden_grad * silu_gate).astype(bf16)

    tok_finish()
    res_finish()
    sent_all(pack_copy)
    for sent in (act_sent, hg_sent, tok_sent, hid_sent, res_sent):
        sent()


def resident_weights_body(tokens, target, w_gate, w_up, w_down_t, kept_blocks):
    n = lax.axis_size("dp")
    mine, width = tokens.shape
    rows = mine * n
    features, channels = w_gate.shape
    kept_count = kept_blocks.shape[0]
    held = kept_count * BLK // n
    wide = -(-held // BLK) * BLK
    pack_rows = -(-2 * mine // 16) * 16
    filler = jnp.zeros((pack_rows - 2 * mine, width), tokens.dtype)
    packed = jnp.concatenate([tokens, target, filler], axis=0)
    bf16, f32 = jnp.bfloat16, jnp.float32
    vmem = pl.BlockSpec(memory_space=pltpu.VMEM)
    hbm = pl.BlockSpec(memory_space=pltpu.HBM)
    small = jax.ShapeDtypeStruct((rows, wide), bf16)
    large = jax.ShapeDtypeStruct((rows, width), bf16)
    picked = kept_count * BLK + BLK
    gate_grad, up_grad, hidden, tok_all, res_all = pl.pallas_call(
        functools.partial(exchange_kernel, n, held),
        out_shape=(small, small, small, large, large),
        in_specs=[pl.BlockSpec(memory_space=pltpu.SMEM), vmem, hbm, hbm, hbm],
        out_specs=(vmem,) * 5,
        scratch_shapes=[
            pltpu.VMEM((features, channels), bf16),
            pltpu.VMEM((features, channels), bf16),
            pltpu.VMEM((features, channels), bf16),
            pltpu.VMEM((n, pack_rows, features), bf16),
            pltpu.VMEM((rows, features), f32),
            pltpu.VMEM((rows, features), f32),
            pltpu.VMEM((rows, features), bf16),
            pltpu.VMEM((2 * rows, channels), f32),
            pltpu.VMEM((2 * rows, picked), f32),
            pltpu.VMEM((features, picked), f32),
            pltpu.VMEM((n, features, wide), bf16),
            pltpu.VMEM((n, 2 * rows, wide), f32),
            pltpu.VMEM((n // 2, 2 * rows, wide), f32),
            pltpu.VMEM((n // 2, 2 * rows, wide), bf16),
            pltpu.VMEM((n // 2, 2 * rows, wide), bf16),
            pltpu.VMEM((rows, wide), bf16),
            pltpu.VMEM((n, rows, wide), bf16),
            pltpu.VMEM((rows, features), bf16),
            pltpu.VMEM((n, rows, wide), f32),
            pltpu.VMEM((n // 2, rows, wide), f32),
            pltpu.VMEM((n // 2, rows, wide), bf16),
            pltpu.VMEM((n // 2, rows, wide), bf16),
            pltpu.SemaphoreType.DMA((3,)),
            pltpu.SemaphoreType.DMA((6, n)),
            pltpu.SemaphoreType.DMA((6, n)),
        ],
        compiler_params=pltpu.CompilerParams(
            collective_id=0, has_side_effects=True, vmem_limit_bytes=58 * 1024 * 1024
        ),
    )(kept_blocks, packed, w_gate, w_up, w_down_t)

    def over_tokens(left, right):
        product = lax.dot_general(
            left, right[:, :held], (((0,), (0,)), ((), ())), preferred_element_type=f32
        )
        return product.astype(bf16)

    return (
        over_tokens(tok_all, gate_grad),
        over_tokens(tok_all, up_grad),
        over_tokens(res_all, hidden),
    )


def body(tokens, target, w_gate, w_up, w_down_t, kept_blocks):
    token_rows = tokens.shape[0] * lax.axis_size("dp")
    few_tokens = token_rows < w_gate.shape[0]
    few_dropped = w_gate.shape[1] // BLK - kept_blocks.shape[0] <= 4
    paired = lax.axis_size("dp") % 2 == 0
    resident = few_tokens and few_dropped and paired
    chosen = resident_weights_body if resident else gathered_weights_body
    return chosen(tokens, target, w_gate, w_up, w_down_t, kept_blocks)


def solution(mesh):
    placed = (
        P(("groups", "dp"), None),
        P(("groups", "dp"), None),
        P("dp", None),
        P("dp", None),
        P("dp", None),
        P(),
    )
    return jax.shard_map(
        body,
        mesh=mesh,
        in_specs=placed,
        out_specs=(P("groups", "dp"), P("groups", "dp"), P("groups", "dp")),
        check_vma=False,
    )
```

```python
import functools

import jax
import jax.numpy as jnp
from jax import lax
from jax.experimental import pallas as pl
from jax.experimental.pallas import tpu as pltpu
from jax.sharding import PartitionSpec as P

BLK = 128


LOSS_SCALE = 16.0


def channel_index(kept_blocks):
    offsets = jnp.arange(BLK, dtype=jnp.int32)
    return (kept_blocks[:, None] * BLK + offsets[None, :]).reshape(-1)


def gathered_weights_body(tokens, target, w_gate, w_up, w_down_t, kept_blocks):
    channels = channel_index(kept_blocks)
    picked_gate = jnp.take(w_gate, channels, axis=1)
    picked_up = jnp.take(w_up, channels, axis=1)
    picked_down = jnp.take(w_down_t, channels, axis=1)
    student_gate, student_up, student_down = (
        lax.all_to_all(picked_gate, "dp", split_axis=1, concat_axis=0, tiled=True),
        lax.all_to_all(picked_up, "dp", split_axis=1, concat_axis=0, tiled=True),
        lax.all_to_all(picked_down, "dp", split_axis=1, concat_axis=0, tiled=True),
    )
    gathered = lax.all_gather(tokens, "dp", axis=0, tiled=True)
    scale = LOSS_SCALE / gathered.shape[0]
    gate_act = jnp.dot(gathered, student_gate, preferred_element_type=jnp.float32)
    up_act = jnp.dot(gathered, student_up, preferred_element_type=jnp.float32)
    sigmoid_gate = jax.nn.sigmoid(gate_act)
    silu_gate = gate_act * sigmoid_gate
    hidden = (silu_gate * up_act).astype(jnp.bfloat16)
    output_rows = lax.psum_scatter(
        lax.dot_general(
            hidden, student_down, (((1,), (1,)), ((), ())), preferred_element_type=jnp.float32
        ),
        "dp",
        scatter_dimension=0,
        tiled=True,
    )
    residual = ((output_rows - target.astype(jnp.float32)) * scale).astype(jnp.bfloat16)
    residual_all = lax.all_gather(residual, "dp", axis=0, tiled=True)
    grad_down = lax.dot_general(
        residual_all, hidden, (((0,), (0,)), ((), ())), preferred_element_type=jnp.float32
    )
    hidden_grad = jnp.dot(residual_all, student_down, preferred_element_type=jnp.float32)
    slope = sigmoid_gate * (1.0 + gate_act * (1.0 - sigmoid_gate))
    gate_grad = (hidden_grad * up_act * slope).astype(jnp.bfloat16)
    up_grad = (hidden_grad * silu_gate).astype(jnp.bfloat16)
    grad_gate = lax.dot_general(
        gathered, gate_grad, (((0,), (0,)), ((), ())), preferred_element_type=jnp.float32
    )
    grad_up = lax.dot_general(
        gathered, up_grad, (((0,), (0,)), ((), ())), preferred_element_type=jnp.float32
    )
    return (
        grad_gate.astype(jnp.bfloat16),
        grad_up.astype(jnp.bfloat16),
        grad_down.astype(jnp.bfloat16),
    )


def exchange_kernel(
    n, held, kept, packed, wg_hbm, wu_hbm, wd_hbm, gate_out, up_out, hid_out, tok_all, res_all,
    wg, wu, wd, packs, tok32, tgt32, tok16, full, sel, down32, down,
    act_out, act_pair, act_sum, act_in, hid16, hid_in, res16, hg_out, hg_pair, hg_sum, hg_in, load_sem, send_sem, recv_sem,
):
    me = lax.axis_index("dp")
    rows, features = tok16.shape
    wide = hid16.shape[1]
    kept_count = kept.shape[0]
    mine = rows // n
    bf16, f32 = jnp.bfloat16, jnp.float32

    loads = [
        pltpu.make_async_copy(src, dst, load_sem.at[i])
        for i, (src, dst) in enumerate(((wg_hbm, wg), (wu_hbm, wu), (wd_hbm, wd)))
    ]
    for load in loads:
        load.start()

    barrier = pltpu.get_barrier_semaphore()

    @pl.loop(1, n)
    def _(k):
        pl.semaphore_signal(
            barrier, inc=1, device_id={"dp": lax.rem(me + k, n)},
            device_id_type=pl.DeviceIdType.MESH,
        )

    pl.semaphore_wait(barrier, n - 1)

    def remote(phase, k, src, dst, to=None):
        return pltpu.make_async_remote_copy(
            src_ref=src, dst_ref=dst, send_sem=send_sem.at[phase, k],
            recv_sem=recv_sem.at[phase, k],
            device_id={"dp": lax.rem(me + k, n) if to is None else to},
            device_id_type=pl.DeviceIdType.MESH,
        )

    chips = n // 2
    sibling = me + 1 - 2 * lax.rem(me, 2)

    def gather_copies(phase, own, slot):
        def across(k):
            return remote(phase, k, own, slot(me), lax.rem(me + 2 * k, n))

        def beside():
            return remote(phase, 0, own, slot(me), sibling)

        def onward(k):
            held_slot = slot(lax.rem(me + n - 2 * k, n))
            return remote(phase, chips + k, held_slot, held_slot, sibling)

        def start():
            @pl.loop(1, chips)
            def _(k):
                across(k).start()

            beside().start()

        def forward(use=lambda i: None):
            @pl.loop(1, chips)
            def _(k):
                across(k).wait_recv()
                onward(k).start()
                use(lax.rem(me + n - 2 * k, n))

        def finish(use=lambda i: None):
            beside().wait_recv()
            use(sibling)

            @pl.loop(1, chips)
            def _(k):
                onward(k).wait_recv()
                use(lax.rem(sibling + n - 2 * k, n))

        def sent():
            beside().wait_send()

            @pl.loop(1, chips)
            def _(k):
                across(k).wait_send()
                onward(k).wait_send()

        return start, forward, finish, sent

    def columns(index):
        return pl.ds(pl.multiple_of(index * features, features), features)

    def pack_copy(k):
        return remote(0, k, packed.at[:, columns(lax.rem(me + k, n))], packs.at[me])

    core = lax.rem(me, 2)
    chip = lax.div(me, 2)

    def sum_copies(phase, out, pair, total, landed):
        def there(k):
            return lax.rem(chip + k, chips)

        def beside(k):
            j = there(k)
            return remote(phase, k, out.at[2 * j + 1 - core], pair.at[j], sibling)

        def across(k):
            j = there(k)
            return remote(phase, chips + k, total.at[j], landed.at[chip], 2 * j + core)

        def combine():
            @pl.loop(1, chips)
            def _(k):
                j = there(k)
                beside(k).wait_recv()
                total[j] = (out[2 * j + core] + pair[j]).astype(bf16)
                across(k).start()

            beside(0).wait_recv()
            landed[chip] = (out[me] + pair[chip]).astype(bf16)

        def finish():
            @pl.loop(1, chips)
            def _(k):
                across(k).wait_recv()

            result = landed[0].astype(f32)
            for s in range(1, chips):
                result = result + landed[s].astype(f32)
            return result

        def sent():
            beside(0).wait_send()

            @pl.loop(1, chips)
            def _(k):
                beside(k).wait_send()
                across(k).wait_send()

        return there, beside, combine, finish, sent

    _, act_beside, act_combine, act_finish, act_sent = sum_copies(
        1, act_out, act_pair, act_sum, act_in
    )
    hg_there, hg_beside, hg_combine, hg_finish, hg_sent = sum_copies(
        4, hg_out, hg_pair, hg_sum, hg_in
    )
    hid_start, hid_forward, hid_finish, hid_sent = gather_copies(
        2, hid16, lambda i: hid_in.at[i]
    )
    res_start, res_forward, res_finish, res_sent = gather_copies(
        3, res16, lambda i: res_all.at[:, columns(i)]
    )
    tok_start, tok_forward, tok_finish, tok_sent = gather_copies(
        5, tok16, lambda i: tok_all.at[:, columns(i)]
    )

    spare = wd.shape[1] // BLK - kept_count

    def kept_block(ref, b):
        shift = jnp.full((ref.shape[0], BLK), kept[b] - b, jnp.int32)
        chosen = ref[:, b * BLK:(b + 1) * BLK].astype(f32)
        for j in range(1, spare + 1):
            other = ref[:, (b + j) * BLK:(b + j + 1) * BLK].astype(f32)
            chosen = jnp.where(shift == j, other, chosen)
        return chosen

    def start_all(copy):
        @pl.loop(1, n)
        def _(k):
            copy(k).start()

    def receive_all(copy):
        @pl.loop(1, n)
        def _(k):
            copy(k).wait_recv()

    def sent_all(copy):
        @pl.loop(1, n)
        def _(k):
            copy(k).wait_send()

    start_all(pack_copy)
    packs[me] = packed[:, columns(me)]
    receive_all(pack_copy)
    for s in range(n):
        piece = packs[s].astype(f32)
        tok32[s * mine:(s + 1) * mine, :] = piece[:mine]
        tgt32[s * mine:(s + 1) * mine, :] = piece[mine:2 * mine]
    tok16[...] = tok32[...].astype(bf16)
    tok_start()

    loads[0].wait()
    loads[1].wait()
    for half, weight in enumerate((wg, wu)):
        here = pl.ds(half * rows, rows)
        for c in range(0, weight.shape[1], 512):
            full[here, c:c + 512] = jnp.dot(
                tok16[...], weight[:, c:c + 512], preferred_element_type=f32
            )
    sel[:, kept_count * BLK:] = jnp.zeros((2 * rows, BLK), f32)
    for b in range(kept_count):
        sel[:, b * BLK:(b + 1) * BLK] = kept_block(full, b)
    for p in range(n):
        act_out[p] = sel[:, p * held:p * held + wide]

        @pl.when(core != p % 2)
        def _(p=p):
            act_beside(lax.rem(p // 2 + chips - chip, chips)).start()

    act_combine()
    tok_all[:, columns(me)] = tok16[...]

    loads[2].wait()
    down32[:, kept_count * BLK:] = jnp.zeros((features, BLK), f32)
    for b in range(kept_count):
        down32[:, b * BLK:(b + 1) * BLK] = kept_block(wd, b)
    for p in range(n):
        down[p] = down32[:, p * held:p * held + wide].astype(bf16)

    tok_forward()
    both = act_finish()
    gate_act, up_act = both[:rows], both[rows:]
    sigmoid_gate = jax.nn.sigmoid(gate_act)
    silu_gate = gate_act * sigmoid_gate
    inside = lax.broadcasted_iota(jnp.int32, (rows, wide), 1) < held
    hidden = jnp.where(inside, silu_gate * up_act, 0.0).astype(bf16)
    hid16[...] = hidden
    hid_out[...] = hidden
    hid_start()
    hid_in[me] = hidden
    tok32[...] = jnp.zeros((rows, features), f32)

    def add_output(s):
        tok32[...] += lax.dot_general(
            hid_in[s], down[s], (((1,), (1,)), ((), ())), preferred_element_type=f32
        )

    add_output(me)
    hid_forward(add_output)
    hid_finish(add_output)

    output = tok32[...]
    residual = ((output_rows - target.astype(jnp.float32)) * scale).astype(jnp.bfloat16)
    residual_all = lax.all_gather(residual, "dp", axis=0, tiled=True)
    grad_down = lax.dot_general(
        residual_all, hidden, (((0,), (0,)), ((), ())), preferred_element_type=jnp.float32
    )
    hidden_grad = jnp.dot(residual_all, student_down, preferred_element_type=jnp.float32)
    slope = sigmoid_gate * (1.0 + gate_act * (1.0 - sigmoid_gate))
    gate_grad = (hidden_grad * up_act * slope).astype(jnp.bfloat16)
    up_grad = (hidden_grad * silu_gate).astype(jnp.bfloat16)
    grad_gate = lax.dot_general(
        gathered, gate_grad, (((0,), (0,)), ((), ())), preferred_element_type=jnp.float32
    )
    grad_up = lax.dot_general(
        gathered, up_grad, (((0,), (0,)), ((), ())), preferred_element_type=jnp.float32
    )
    return (
        grad_gate.astype(jnp.bfloat16),
        grad_up.astype(jnp.bfloat16),
        grad_down.astype(jnp.bfloat16),
    )


def exchange_kernel(
    n, held, kept, packed, wg_hbm, wu_hbm, wd_hbm, gate_out, up_out, hid_out, tok_all, res_all,
    wg, wu, wd, packs, tok32, tgt32, tok16, full, sel, down32, down,
    act_out, act_pair, act_sum, act_in, hid16, hid_in, res16, hg_out, hg_pair, hg_sum, hg_in, load_sem, send_sem, recv_sem,
):
    me = lax.axis_index("dp")
    rows, features = tok16.shape
    wide = hid16.shape[1]
    kept_count = kept.shape[0]
    mine = rows // n
    bf16, f32 = jnp.bfloat16, jnp.float32

    loads = [
        pltpu.make_async_copy(src, dst, load_sem.at[i])
        for i, (src, dst) in enumerate(((wg_hbm, wg), (wu_hbm, wu), (wd_hbm, wd)))
    ]
    for load in loads:
        load.start()

    barrier = pltpu.get_barrier_semaphore()

    @pl.loop(1, n)
    def _(k):
        pl.semaphore_signal(
            barrier, inc=1, device_id={"dp": lax.rem(me + k, n)},
            device_id_type=pl.DeviceIdType.MESH,
        )

    pl.semaphore_wait(barrier, n - 1)

    def remote(phase, k, src, dst, to=None):
        return pltpu.make_async_remote_copy(
            src_ref=src, dst_ref=dst, send_sem=send_sem.at[phase, k],
            recv_sem=recv_sem.at[phase, k],
            device_id={"dp": lax.rem(me + k, n) if to is None else to},
            device_id_type=pl.DeviceIdType.MESH,
        )

    chips = n // 2
    sibling = me + 1 - 2 * lax.rem(me, 2)

    def gather_copies(phase, own, slot):
        def across(k):
            return remote(phase, k, own, slot(me), lax.rem(me + 2 * k, n))

        def beside():
            return remote(phase, 0, own, slot(me), sibling)

        def onward(k):
            held_slot = slot(lax.rem(me + n - 2 * k, n))
            return remote(phase, chips + k, held_slot, held_slot, sibling)

        def start():
            @pl.loop(1, chips)
            def _(k):
                across(k).start()

            beside().start()

        def forward(use=lambda i: None):
            @pl.loop(1, chips)
            def _(k):
                across(k).wait_recv()
                onward(k).start()
                use(lax.rem(me + n - 2 * k, n))

        def finish(use=lambda i: None):
            beside().wait_recv()
            use(sibling)

            @pl.loop(1, chips)
            def _(k):
                onward(k).wait_recv()
                use(lax.rem(sibling + n - 2 * k, n))

        def sent():
            beside().wait_send()

            @pl.loop(1, chips)
            def _(k):
                across(k).wait_send()
                onward(k).wait_send()

        return start, forward, finish, sent

    def columns(index):
        return pl.ds(pl.multiple_of(index * features, features), features)

    def pack_copy(k):
        return remote(0, k, packed.at[:, columns(lax.rem(me + k, n))], packs.at[me])

    core = lax.rem(me, 2)
    chip = lax.div(me, 2)

    def sum_copies(phase, out, pair, total, landed):
        def there(k):
            return lax.rem(chip + k, chips)

        def beside(k):
            j = there(k)
            return remote(phase, k, out.at[2 * j + 1 - core], pair.at[j], sibling)

        def across(k):
            j = there(k)
            return remote(phase, chips + k, total.at[j], landed.at[chip], 2 * j + core)

        def combine():
            @pl.loop(1, chips)
            def _(k):
                j = there(k)
                beside(k).wait_recv()
                total[j] = (out[2 * j + core] + pair[j]).astype(bf16)
                across(k).start()

            beside(0).wait_recv()
            landed[chip] = (out[me] + pair[chip]).astype(bf16)

        def finish():
            @pl.loop(1, chips)
            def _(k):
                across(k).wait_recv()

            result = landed[0].astype(f32)
            for s in range(1, chips):
                result = result + landed[s].astype(f32)
            return result

        def sent():
            beside(0).wait_send()

            @pl.loop(1, chips)
            def _(k):
                beside(k).wait_send()
                across(k).wait_send()

        return there, beside, combine, finish, sent

    _, act_beside, act_combine, act_finish, act_sent = sum_copies(
        1, act_out, act_pair, act_sum, act_in
    )
    hg_there, hg_beside, hg_combine, hg_finish, hg_sent = sum_copies(
        4, hg_out, hg_pair, hg_sum, hg_in
    )
    hid_start, hid_forward, hid_finish, hid_sent = gather_copies(
        2, hid16, lambda i: hid_in.at[i]
    )
    res_start, res_forward, res_finish, res_sent = gather_copies(
        3, res16, lambda i: res_all.at[:, columns(i)]
    )
    tok_start, tok_forward, tok_finish, tok_sent = gather_copies(
        5, tok16, lambda i: tok_all.at[:, columns(i)]
    )

    spare = wd.shape[1] // BLK - kept_count

    def kept_block(ref, b):
        shift = jnp.full((ref.shape[0], BLK), kept[b] - b, jnp.int32)
        chosen = ref[:, b * BLK:(b + 1) * BLK].astype(f32)
        for j in range(1, spare + 1):
            other = ref[:, (b + j) * BLK:(b + j + 1) * BLK].astype(f32)
            chosen = jnp.where(shift == j, other, chosen)
        return chosen

    def start_all(copy):
        @pl.loop(1, n)
        def _(k):
            copy(k).start()

    def receive_all(copy):
        @pl.loop(1, n)
        def _(k):
            copy(k).wait_recv()

    def sent_all(copy):
        @pl.loop(1, n)
        def _(k):
            copy(k).wait_send()

    start_all(pack_copy)
    packs[me] = packed[:, columns(me)]
    receive_all(pack_copy)
    for s in range(n):
        piece = packs[s].astype(f32)
        tok32[s * mine:(s + 1) * mine, :] = piece[:mine]
        tgt32[s * mine:(s + 1) * mine, :] = piece[mine:2 * mine]
    tok16[...] = tok32[...].astype(bf16)
    tok_start()

    loads[0].wait()
    loads[1].wait()
    for half, weight in enumerate((wg, wu)):
        here = pl.ds(half * rows, rows)
        for c in range(0, weight.shape[1], 512):
            full[here, c:c + 512] = jnp.dot(
                tok16[...], weight[:, c:c + 512], preferred_element_type=f32
            )
    sel[:, kept_count * BLK:] = jnp.zeros((2 * rows, BLK), f32)
    for b in range(kept_count):
        sel[:, b * BLK:(b + 1) * BLK] = kept_block(full, b)
    for p in range(n):
        act_out[p] = sel[:, p * held:p * held + wide]

    @pl.loop(1, chips)
    def _(k):
        act_beside(k).start()

    act_beside(0).start()
    act_combine()
    tok_all[:, columns(me)] = tok16[...]

    loads[2].wait()
    down32[:, kept_count * BLK:] = jnp.zeros((features, BLK), f32)
    for b in range(kept_count):
        down32[:, b * BLK:(b + 1) * BLK] = kept_block(wd, b)
    for p in range(n):
        down[p] = down32[:, p * held:p * held + wide].astype(bf16)

    tok_forward()
    both = act_finish()
    gate_act, up_act = both[:rows], both[rows:]
    sigmoid_gate = jax.nn.sigmoid(gate_act)
    silu_gate = gate_act * sigmoid_gate
    inside = lax.broadcasted_iota(jnp.int32, (rows, wide), 1) < held
    hidden = jnp.where(inside, silu_gate * up_act, 0.0).astype(bf16)
    hid16[...] = hidden
    hid_out[...] = hidden
    hid_start()
    hid_in[me] = hidden
    tok32[...] = jnp.zeros((rows, features), f32)

    def add_output(s):
        tok32[...] += lax.dot_general(
            hid_in[s], down[s], (((1,), (1,)), ((), ())), preferred_element_type=f32
        )

    add_output(me)
    hid_forward(add_output)
    hid_finish(add_output)

    output = jnp.zeros((rows, features), f32)
    for s in range(n):
        output = output + lax.dot_general(
            hid_in[s], down[s], (((1,), (1,)), ((), ())), preferred_element_type=f32
        )
    residual = ((output - tgt32[...]) * (LOSS_SCALE / rows)).astype(bf16)
    res16[...] = residual

    def hg_piece(p):
        hg_out[p] = jnp.dot(res16[...], down[p], preferred_element_type=f32)

    @pl.loop(1, chips + 1)
    def _(step):
        k = lax.rem(step, chips)
        hg_piece(2 * hg_there(k) + 1 - core)
        hg_beside(k).start()

    @pl.loop(0, chips)
    def _(k):
        hg_piece(2 * hg_there(k) + core)

    hg_combine()
    res_start()
    res_all[:, columns(me)] = residual
    res_forward()
    hidden_grad = hg_finish()
    slope = sigmoid_gate * (1.0 + gate_act * (1.0 - sigmoid_gate))
    gate_out[...] = (hidden_grad * up_act * slope).astype(bf16)
    up_out[...] = (hidden_grad * silu_gate).astype(bf16)

    tok_finish()
    res_finish()
    sent_all(pack_copy)
    for sent in (act_sent, hg_sent, tok_sent, hid_sent, res_sent):
        sent()


def resident_weights_body(tokens, target, w_gate, w_up, w_down_t, kept_blocks):
    n = lax.axis_size("dp")
    mine, width = tokens.shape
    rows = mine * n
    features, channels = w_gate.shape
    kept_count = kept_blocks.shape[0]
    held = kept_count * BLK // n
    wide = -(-held // BLK) * BLK
    pack_rows = -(-2 * mine // 16) * 16
    filler = jnp.zeros((pack_rows - 2 * mine, width), tokens.dtype)
    packed = jnp.concatenate([tokens, target, filler], axis=0)
    bf16, f32 = jnp.bfloat16, jnp.float32
    vmem = pl.BlockSpec(memory_space=pltpu.VMEM)
    hbm = pl.BlockSpec(memory_space=pltpu.HBM)
    small = jax.ShapeDtypeStruct((rows, wide), bf16)
    large = jax.ShapeDtypeStruct((rows, width), bf16)
    picked = kept_count * BLK + BLK
    gate_grad, up_grad, hidden, tok_all, res_all = pl.pallas_call(
        functools.partial(exchange_kernel, n, held),
        out_shape=(small, small, small, large, large),
        in_specs=[pl.BlockSpec(memory_space=pltpu.SMEM), vmem, hbm, hbm, hbm],
        out_specs=(vmem,) * 5,
        scratch_shapes=[
            pltpu.VMEM((features, channels), bf16),
            pltpu.VMEM((features, channels), bf16),
            pltpu.VMEM((features, channels), bf16),
            pltpu.VMEM((n, pack_rows, features), bf16),
            pltpu.VMEM((rows, features), f32),
            pltpu.VMEM((rows, features), f32),
            pltpu.VMEM((rows, features), bf16),
            pltpu.VMEM((2 * rows, channels), f32),
            pltpu.VMEM((2 * rows, picked), f32),
            pltpu.VMEM((features, picked), f32),
            pltpu.VMEM((n, features, wide), bf16),
            pltpu.VMEM((n, 2 * rows, wide), f32),
            pltpu.VMEM((n // 2, 2 * rows, wide), f32),
            pltpu.VMEM((n // 2, 2 * rows, wide), bf16),
            pltpu.VMEM((n // 2, 2 * rows, wide), bf16),
            pltpu.VMEM((rows, wide), bf16),
            pltpu.VMEM((n, rows, wide), bf16),
            pltpu.VMEM((rows, features), bf16),
            pltpu.VMEM((n, rows, wide), f32),
            pltpu.VMEM((n // 2, rows, wide), f32),
            pltpu.VMEM((n // 2, rows, wide), bf16),
            pltpu.VMEM((n // 2, rows, wide), bf16),
            pltpu.SemaphoreType.DMA((3,)),
            pltpu.SemaphoreType.DMA((6, n)),
            pltpu.SemaphoreType.DMA((6, n)),
        ],
        compiler_params=pltpu.CompilerParams(
            collective_id=0, has_side_effects=True, vmem_limit_bytes=58 * 1024 * 1024
        ),
    )(kept_blocks, packed, w_gate, w_up, w_down_t)

    def over_tokens(left, right):
        product = lax.dot_general(
            left, right[:, :held], (((0,), (0,)), ((), ())), preferred_element_type=f32
        )
        return product.astype(bf16)

    return (
        over_tokens(tok_all, gate_grad),
        over_tokens(tok_all, up_grad),
        over_tokens(res_all, hidden),
    )


def body(tokens, target, w_gate, w_up, w_down_t, kept_blocks):
    token_rows = tokens.shape[0] * lax.axis_size("dp")
    few_tokens = token_rows < w_gate.shape[0]
    few_dropped = w_gate.shape[1] // BLK - kept_blocks.shape[0] <= 4
    paired = lax.axis_size("dp") % 2 == 0
    resident = few_tokens and few_dropped and paired
    chosen = resident_weights_body if resident else gathered_weights_body
    return chosen(tokens, target, w_gate, w_up, w_down_t, kept_blocks)


def solution(mesh):
    placed = (
        P(("groups", "dp"), None),
        P(("groups", "dp"), None),
        P("dp", None),
        P("dp", None),
        P("dp", None),
        P(),
    )
    return jax.shard_map(
        body,
        mesh=mesh,
        in_specs=placed,
        out_specs=(P("groups", "dp"), P("groups", "dp"), P("groups", "dp")),
        check_vma=False,
    )
```

```python
import functools

import jax
import jax.numpy as jnp
from jax import lax
from jax.experimental import pallas as pl
from jax.experimental.pallas import tpu as pltpu
from jax.sharding import PartitionSpec as P

BLK = 128


LOSS_SCALE = 16.0


def channel_index(kept_blocks):
    offsets = jnp.arange(BLK, dtype=jnp.int32)
    return (kept_blocks[:, None] * BLK + offsets[None, :]).reshape(-1)


def gathered_weights_body(tokens, target, w_gate, w_up, w_down_t, kept_blocks):
    channels = channel_index(kept_blocks)
    picked_gate = jnp.take(w_gate, channels, axis=1)
    picked_up = jnp.take(w_up, channels, axis=1)
    picked_down = jnp.take(w_down_t, channels, axis=1)
    student_gate, student_up, student_down = (
        lax.all_to_all(picked_gate, "dp", split_axis=1, concat_axis=0, tiled=True),
        lax.all_to_all(picked_up, "dp", split_axis=1, concat_axis=0, tiled=True),
        lax.all_to_all(picked_down, "dp", split_axis=1, concat_axis=0, tiled=True),
    )
    gathered = lax.all_gather(tokens, "dp", axis=0, tiled=True)
    scale = LOSS_SCALE / gathered.shape[0]
    gate_act = jnp.dot(gathered, student_gate, preferred_element_type=jnp.float32)
    up_act = jnp.dot(gathered, student_up, preferred_element_type=jnp.float32)
    sigmoid_gate = jax.nn.sigmoid(gate_act)
    silu_gate = gate_act * sigmoid_gate
    hidden = (silu_gate * up_act).astype(jnp.bfloat16)
    output_rows = lax.psum_scatter(
        lax.dot_general(
            hidden, student_down, (((1,), (1,)), ((), ())), preferred_element_type=jnp.float32
        ),
        "dp",
        scatter_dimension=0,
        tiled=True,
    )
    residual = ((output_rows - target.astype(jnp.float32)) * scale).astype(jnp.bfloat16)
    residual_all = lax.all_gather(residual, "dp", axis=0, tiled=True)
    grad_down = lax.dot_general(
        residual_all, hidden, (((0,), (0,)), ((), ())), preferred_element_type=jnp.float32
    )
    hidden_grad = jnp.dot(residual_all, student_down, preferred_element_type=jnp.float32)
    slope = sigmoid_gate * (1.0 + gate_act * (1.0 - sigmoid_gate))
    gate_grad = (hidden_grad * up_act * slope).astype(jnp.bfloat16)
    up_grad = (hidden_grad * silu_gate).astype(jnp.bfloat16)
    grad_gate = lax.dot_general(
        gathered, gate_grad, (((0,), (0,)), ((), ())), preferred_element_type=jnp.float32
    )
    grad_up = lax.dot_general(
        gathered, up_grad, (((0,), (0,)), ((), ())), preferred_element_type=jnp.float32
    )
    return (
        grad_gate.astype(jnp.bfloat16),
        grad_up.astype(jnp.bfloat16),
        grad_down.astype(jnp.bfloat16),
    )


def exchange_kernel(
    n, held, kept, packed, wg_hbm, wu_hbm, wd_hbm, gate_out, up_out, hid_out, tok_all, res_all,
    wg, wu, wd, packs, tok32, tgt32, tok16, full, sel, down32, down,
    act_out, act_pair, act_sum, act_in, hid16, hid_in, res16, hg_out, hg_pair, hg_sum, hg_in, load_sem, send_sem, recv_sem,
):
    me = lax.axis_index("dp")
    rows, features = tok16.shape
    wide = hid16.shape[1]
    kept_count = kept.shape[0]
    mine = rows // n
    bf16, f32 = jnp.bfloat16, jnp.float32

    loads = [
        pltpu.make_async_copy(src, dst, load_sem.at[i])
        for i, (src, dst) in enumerate(((wg_hbm, wg), (wu_hbm, wu), (wd_hbm, wd)))
    ]
    for load in loads:
        load.start()

    barrier = pltpu.get_barrier_semaphore()

    @pl.loop(1, n)
    def _(k):
        pl.semaphore_signal(
            barrier, inc=1, device_id={"dp": lax.rem(me + k, n)},
            device_id_type=pl.DeviceIdType.MESH,
        )

    pl.semaphore_wait(barrier, n - 1)

    def remote(phase, k, src, dst, to=None):
        return pltpu.make_async_remote_copy(
            src_ref=src, dst_ref=dst, send_sem=send_sem.at[phase, k],
            recv_sem=recv_sem.at[phase, k],
            device_id={"dp": lax.rem(me + k, n) if to is None else to},
            device_id_type=pl.DeviceIdType.MESH,
        )

    chips = n // 2
    sibling = me + 1 - 2 * lax.rem(me, 2)

    def gather_copies(phase, own, slot):
        def across(k):
            return remote(phase, k, own, slot(me), lax.rem(me + 2 * k, n))

        def beside():
            return remote(phase, 0, own, slot(me), sibling)

        def onward(k):
            held_slot = slot(lax.rem(me + n - 2 * k, n))
            return remote(phase, chips + k, held_slot, held_slot, sibling)

        def start():
            @pl.loop(1, chips)
            def _(k):
                across(k).start()

            beside().start()

        def forward():
            @pl.loop(1, chips)
            def _(k):
                across(k).wait_recv()
                onward(k).start()

        def finish():
            beside().wait_recv()

            @pl.loop(1, chips)
            def _(k):
                onward(k).wait_recv()

        def sent():
            beside().wait_send()

            @pl.loop(1, chips)
            def _(k):
                across(k).wait_send()
                onward(k).wait_send()

        return start, forward, finish, sent

    def columns(index):
        return pl.ds(pl.multiple_of(index * features, features), features)

    def pack_copy(k):
        return remote(0, k, packed.at[:, columns(lax.rem(me + k, n))], packs.at[me])

    core = lax.rem(me, 2)
    chip = lax.div(me, 2)

    def sum_copies(phase, out, pair, total, landed):
        def there(k):
            return lax.rem(chip + k, chips)

        def beside(k):
            j = there(k)
            return remote(phase, k, out.at[2 * j + 1 - core], pair.at[j], sibling)

        def across(k):
            j = there(k)
            return remote(phase, chips + k, total.at[j], landed.at[chip], 2 * j + core)

        def combine(prepare=lambda i: None):
            @pl.loop(1, chips)
            def _(k):
                j = there(k)
                prepare(2 * j + core)
                beside(k).wait_recv()
                total[j] = (out[2 * j + core] + pair[j]).astype(bf16)
                across(k).start()

            prepare(me)
            beside(0).wait_recv()
            landed[chip] = (out[me] + pair[chip]).astype(bf16)

        def finish():
            @pl.loop(1, chips)
            def _(k):
                across(k).wait_recv()

            result = landed[0].astype(f32)
            for s in range(1, chips):
                result = result + landed[s].astype(f32)
            return result

        def sent():
            beside(0).wait_send()

            @pl.loop(1, chips)
            def _(k):
                beside(k).wait_send()
                across(k).wait_send()

        return there, beside, combine, finish, sent

    _, act_beside, act_combine, act_finish, act_sent = sum_copies(
        1, act_out, act_pair, act_sum, act_in
    )
    hg_there, hg_beside, hg_combine, hg_finish, hg_sent = sum_copies(
        4, hg_out, hg_pair, hg_sum, hg_in
    )
    hid_start, hid_forward, hid_finish, hid_sent = gather_copies(
        2, hid16, lambda i: hid_in.at[i]
    )
    res_start, res_forward, res_finish, res_sent = gather_copies(
        3, res16, lambda i: res_all.at[:, columns(i)]
    )
    tok_start, tok_forward, tok_finish, tok_sent = gather_copies(
        5, tok16, lambda i: tok_all.at[:, columns(i)]
    )

    spare = wd.shape[1] // BLK - kept_count

    def kept_block(ref, b):
        shift = jnp.full((ref.shape[0], BLK), kept[b] - b, jnp.int32)
        chosen = ref[:, b * BLK:(b + 1) * BLK].astype(f32)
        for j in range(1, spare + 1):
            other = ref[:, (b + j) * BLK:(b + j + 1) * BLK].astype(f32)
            chosen = jnp.where(shift == j, other, chosen)
        return chosen

    def start_all(copy):
        @pl.loop(1, n)
        def _(k):
            copy(k).start()

    def receive_all(copy):
        @pl.loop(1, n)
        def _(k):
            copy(k).wait_recv()

    def sent_all(copy):
        @pl.loop(1, n)
        def _(k):
            copy(k).wait_send()

    start_all(pack_copy)
    packs[me] = packed[:, columns(me)]
    receive_all(pack_copy)
    for s in range(n):
        piece = packs[s].astype(f32)
        tok32[s * mine:(s + 1) * mine, :] = piece[:mine]
        tgt32[s * mine:(s + 1) * mine, :] = piece[mine:2 * mine]
    tok16[...] = tok32[...].astype(bf16)
    tok_start()

    loads[0].wait()
    loads[1].wait()
    for half, weight in enumerate((wg, wu)):
        here = pl.ds(half * rows, rows)
        for c in range(0, weight.shape[1], 512):
            full[here, c:c + 512] = jnp.dot(
                tok16[...], weight[:, c:c + 512], preferred_element_type=f32
            )
    sel[:, kept_count * BLK:] = jnp.zeros((2 * rows, BLK), f32)
    for b in range(kept_count):
        sel[:, b * BLK:(b + 1) * BLK] = kept_block(full, b)
    for p in range(n):
        act_out[p] = sel[:, p * held:p * held + wide]

    @pl.loop(1, chips)
    def _(k):
        act_beside(k).start()

    act_beside(0).start()
    act_combine()
    tok_all[:, columns(me)] = tok16[...]

    loads[2].wait()
    down32[:, kept_count * BLK:] = jnp.zeros((features, BLK), f32)
    for b in range(kept_count):
        down32[:, b * BLK:(b + 1) * BLK] = kept_block(wd, b)
    for p in range(n):
        down[p] = down32[:, p * held:p * held + wide].astype(bf16)

    tok_forward()
    both = act_finish()
    gate_act, up_act = both[:rows], both[rows:]
    sigmoid_gate = jax.nn.sigmoid(gate_act)
    silu_gate = gate_act * sigmoid_gate
    inside = lax.broadcasted_iota(jnp.int32, (rows, wide), 1) < held
    hidden = jnp.where(inside, silu_gate * up_act, 0.0).astype(bf16)
    hid16[...] = hidden
    hid_out[...] = hidden
    hid_start()
    hid_in[me] = hidden
    hid_forward()
    hid_finish()

    output = jnp.zeros((rows, features), f32)
    for s in range(n):
        output = output + lax.dot_general(
            hid_in[s], down[s], (((1,), (1,)), ((), ())), preferred_element_type=f32
        )
    residual = ((output - tgt32[...]) * (LOSS_SCALE / rows)).astype(bf16)
    res16[...] = residual

    def hg_piece(p):
        hg_out[p] = jnp.dot(res16[...], down[p], preferred_element_type=f32)

    @pl.loop(1, chips + 1)
    def _(step):
        k = lax.rem(step, chips)
        hg_piece(2 * hg_there(k) + 1 - core)
        hg_beside(k).start()

    hg_combine(hg_piece)
    res_start()
    res_all[:, columns(me)] = residual
    res_forward()
    hidden_grad = hg_finish()
    slope = sigmoid_gate * (1.0 + gate_act * (1.0 - sigmoid_gate))
    gate_out[...] = (hidden_grad * up_act * slope).astype(bf16)
    up_out[...] = (hidden_grad * silu_gate).astype(bf16)

    tok_finish()
    res_finish()
    sent_all(pack_copy)
    for sent in (act_sent, hg_sent, tok_sent, hid_sent, res_sent):
        sent()


def resident_weights_body(tokens, target, w_gate, w_up, w_down_t, kept_blocks):
    n = lax.axis_size("dp")
    mine, width = tokens.shape
    rows = mine * n
    features, channels = w_gate.shape
    kept_count = kept_blocks.shape[0]
    held = kept_count * BLK // n
    wide = -(-held // BLK) * BLK
    pack_rows = -(-2 * mine // 16) * 16
    filler = jnp.zeros((pack_rows - 2 * mine, width), tokens.dtype)
    packed = jnp.concatenate([tokens, target, filler], axis=0)
    bf16, f32 = jnp.bfloat16, jnp.float32
    vmem = pl.BlockSpec(memory_space=pltpu.VMEM)
    hbm = pl.BlockSpec(memory_space=pltpu.HBM)
    small = jax.ShapeDtypeStruct((rows, wide), bf16)
    large = jax.ShapeDtypeStruct((rows, width), bf16)
    picked = kept_count * BLK + BLK
    gate_grad, up_grad, hidden, tok_all, res_all = pl.pallas_call(
        functools.partial(exchange_kernel, n, held),
        out_shape=(small, small, small, large, large),
        in_specs=[pl.BlockSpec(memory_space=pltpu.SMEM), vmem, hbm, hbm, hbm],
        out_specs=(vmem,) * 5,
        scratch_shapes=[
            pltpu.VMEM((features, channels), bf16),
            pltpu.VMEM((features, channels), bf16),
            pltpu.VMEM((features, channels), bf16),
            pltpu.VMEM((n, pack_rows, features), bf16),
            pltpu.VMEM((rows, features), f32),
            pltpu.VMEM((rows, features), f32),
            pltpu.VMEM((rows, features), bf16),
            pltpu.VMEM((2 * rows, channels), f32),
            pltpu.VMEM((2 * rows, picked), f32),
            pltpu.VMEM((features, picked), f32),
            pltpu.VMEM((n, features, wide), bf16),
            pltpu.VMEM((n, 2 * rows, wide), f32),
            pltpu.VMEM((n // 2, 2 * rows, wide), f32),
            pltpu.VMEM((n // 2, 2 * rows, wide), bf16),
            pltpu.VMEM((n // 2, 2 * rows, wide), bf16),
            pltpu.VMEM((rows, wide), bf16),
            pltpu.VMEM((n, rows, wide), bf16),
            pltpu.VMEM((rows, features), bf16),
            pltpu.VMEM((n, rows, wide), f32),
            pltpu.VMEM((n // 2, rows, wide), f32),
            pltpu.VMEM((n // 2, rows, wide), bf16),
            pltpu.VMEM((n // 2, rows, wide), bf16),
            pltpu.SemaphoreType.DMA((3,)),
            pltpu.SemaphoreType.DMA((6, n)),
            pltpu.SemaphoreType.DMA((6, n)),
        ],
        compiler_params=pltpu.CompilerParams(
            collective_id=0, has_side_effects=True, vmem_limit_bytes=58 * 1024 * 1024
        ),
    )(kept_blocks, packed, w_gate, w_up, w_down_t)

    def over_tokens(left, right):
        product = lax.dot_general(
            left, right[:, :held], (((0,), (0,)), ((), ())), preferred_element_type=f32
        )
        return product.astype(bf16)

    return (
        over_tokens(tok_all, gate_grad),
        over_tokens(tok_all, up_grad),
        over_tokens(res_all, hidden),
    )


def body(tokens, target, w_gate, w_up, w_down_t, kept_blocks):
    token_rows = tokens.shape[0] * lax.axis_size("dp")
    few_tokens = token_rows < w_gate.shape[0]
    few_dropped = w_gate.shape[1] // BLK - kept_blocks.shape[0] <= 4
    paired = lax.axis_size("dp") % 2 == 0
    resident = few_tokens and few_dropped and paired
    chosen = resident_weights_body if resident else gathered_weights_body
    return chosen(tokens, target, w_gate, w_up, w_down_t, kept_blocks)


def solution(mesh):
    placed = (
        P(("groups", "dp"), None),
        P(("groups", "dp"), None),
        P("dp", None),
        P("dp", None),
        P("dp", None),
        P(),
    )
    return jax.shard_map(
        body,
        mesh=mesh,
        in_specs=placed,
        out_specs=(P("groups", "dp"), P("groups", "dp"), P("groups", "dp")),
        check_vma=False,
    )
```
